32 devices in a mesh: ta: 4 (over y, core), gx: 8 (over z, x).
Axes of the slice: x: 2, y: 2, z: 4, core: 2. Of those that a mesh axis runs over, the one named last changes fastest.
Arguments:
- links: float32 [4, 2, 3, 3, 64, 16, 128], P(None, None, None, None, 'ta', 'gx'), may hold values from -1 to 1, as said below
Outputs:
- flowed: float32 [4, 2, 3, 3, 64, 16, 128], P(None, None, None, None, 'ta', 'gx')
- loop_table: float32 [5, 8], replicated
The draws below stay inside these ranges and needn't reach their ends.
Inputs may be any that keep to these rules, and one draw needn't show every extreme that they name: `links`: every link is a special unitary 3 x 3 matrix, given by its real and imaginary parts.
All inputs are finite; a program needn't handle non-finite values.
Results may differ from the reference program's by a relative error of at most 0.0001.
Values sent between devices are 32-bit elements; how exact they have to be, the bound alone decides.
A program may use at most 192 MiB of HBM per device.

```python
import jax
import jax.numpy as jnp

NY = 4
NZ = 32
TMAX = 8
LEVELS = 5
NT = 64
NX = 16


def complex_product_drawn(a, b):
    real_part = jnp.sum(a[0][:, :, None] * b[0][None], axis=1) - jnp.sum(a[1][:, :, None] * b[1][None], axis=1)
    imag_part = jnp.sum(a[0][:, :, None] * b[1][None], axis=1) + jnp.sum(a[1][:, :, None] * b[0][None], axis=1)
    return jnp.stack([real_part, imag_part])


def embedding(quaternion, leading, second):
    zeros_field = jnp.zeros_like(quaternion[0])
    ones_field = jnp.ones_like(quaternion[0])
    real_part = [[ones_field if i == j else zeros_field for j in range(3)] for i in range(3)]
    imag_part = [[zeros_field for j in range(3)] for i in range(3)]
    real_part[leading][leading] = quaternion[0]
    imag_part[leading][leading] = quaternion[3]
    real_part[second][second] = quaternion[0]
    imag_part[second][second] = -quaternion[3]
    real_part[leading][second] = quaternion[2]
    imag_part[leading][second] = quaternion[1]
    real_part[second][leading] = -quaternion[2]
    imag_part[second][leading] = quaternion[1]
    stacked_real = jnp.stack([jnp.stack(entries) for entries in real_part])
    stacked_imag = jnp.stack([jnp.stack(entries) for entries in imag_part])
    return jnp.stack([stacked_real, stacked_imag])


def draw_links(key, part):
    key = jax.random.fold_in(key, 11)
    extents = (4, 4, NT, NX, NY * NZ)
    factors = []
    for position, planes in enumerate(((0, 1), (1, 2), (0, 2))):
        subkey = jax.random.fold_in(key, position)
        quaternion = 0.08 * jax.random.normal(subkey, extents, jnp.float32)
        quaternion = jnp.concatenate([1.0 + quaternion[:1], quaternion[1:]])
        quaternion = quaternion / jnp.sqrt(jnp.sum(quaternion * quaternion, 0))
        factors.append(embedding(quaternion, planes[0], planes[1]))
    result = complex_product_drawn(complex_product_drawn(factors[0], factors[1]), factors[2])
    return jnp.moveaxis(result, 3, 0).astype(jnp.float32)


def setup_inputs(seed: int = 0) -> dict:
    streams_of = jax.random.split(jax.random.key(seed), 2)
    links = draw_links(jax.random.fold_in(streams_of[1], 71), 0)
    return dict(links=links)


EPS_FLOW = 0.05
series_terms = 6


def complex_product(a, b):
    real_part = jnp.sum(a[0][:, :, None] * b[0][None], axis=1) - jnp.sum(a[1][:, :, None] * b[1][None], axis=1)
    imag_part = jnp.sum(a[0][:, :, None] * b[1][None], axis=1) + jnp.sum(a[1][:, :, None] * b[0][None], axis=1)
    return jnp.stack([real_part, imag_part])


def dagger(a):
    return jnp.stack([jnp.swapaxes(a[0], 0, 1), -jnp.swapaxes(a[1], 0, 1)])


def real_trace(a, b):
    return jnp.sum(a[0] * b[0] + a[1] * b[1])


def neighbour(matrices, direction, offset):
    if direction == 0:
        return jnp.roll(matrices, -offset, axis=matrices.ndim - 3)
    if direction == 1:
        return jnp.roll(matrices, -offset, axis=matrices.ndim - 2)
    if direction == 2:
        return jnp.roll(matrices, -offset * NZ, axis=matrices.ndim - 1)
    planes = matrices.reshape(matrices.shape[:-1] + (NY, NZ))
    return jnp.roll(planes, -offset, axis=planes.ndim - 1).reshape(matrices.shape)


def project(plaquettes):
    real_part = 0.5 * (plaquettes[0] - jnp.swapaxes(plaquettes[0], 0, 1))
    imag_part = 0.5 * (plaquettes[1] + jnp.swapaxes(plaquettes[1], 0, 1))
    trace_part = (imag_part[0, 0] + imag_part[1, 1] + imag_part[2, 2]) / 3.0
    identity = jnp.eye(3, dtype=imag_part.dtype).reshape((3, 3) + (1,) * (imag_part.ndim - 2))
    return jnp.stack([real_part, imag_part - identity * trace_part])


def exponential(generator):
    identity = jnp.eye(3, dtype=generator.dtype).reshape((3, 3) + (1,) * (generator.ndim - 3))
    unit = jnp.stack([identity + jnp.zeros_like(generator[0]), jnp.zeros_like(generator[1])])
    result = unit
    for k in range(series_terms, 0, -1):
        result = unit + complex_product(generator, result) / k
    return result


def flow_step(links, interior):
    flowed_list = []
    for direction in range(4):
        summed = None
        for across in [v for v in range(4) if v != direction]:
            upper_term = complex_product(complex_product(interior(neighbour(links[across], direction, 1)), dagger(interior(neighbour(links[direction], across, 1)))), dagger(interior(links[across])))
            lowered = neighbour(links[across], across, -1)
            lower_term = complex_product(complex_product(dagger(interior(neighbour(lowered, direction, 1))), dagger(interior(neighbour(links[direction], across, -1)))), interior(lowered))
            summed = upper_term + lower_term if summed is None else summed + upper_term + lower_term
        plaquettes = complex_product(interior(links[direction]), summed)
        generator = -EPS_FLOW * project(plaquettes)
        flowed_list.append(complex_product(exponential(generator), interior(links[direction])))
    return jnp.stack(flowed_list)


def wilson_loops(spatial, ahead_by, time_source, shifted_source, spatial_source):
    carried = spatial
    values = []
    for extent in range(1, TMAX + 1):
        carried = complex_product(complex_product(dagger(ahead_by(time_source, extent - 1)), carried), ahead_by(shifted_source, extent - 1))
        values.append(real_trace(carried, ahead_by(spatial_source, extent)))
    return jnp.stack(values)


def reference(links):
    flowed = flow_step(links, lambda f: f)
    time_links, x_links = flowed[0], flowed[1]
    ahead_by = lambda f, s: neighbour(f, 0, s)
    spatial = x_links
    shifted = neighbour(time_links, 1, 1)
    distance = 1
    entries = []
    for k in range(LEVELS):
        entries.append(wilson_loops(spatial, ahead_by, time_links, shifted, spatial))
        if k + 1 < LEVELS:
            spatial = complex_product(spatial, neighbour(spatial, 1, distance))
            shifted = neighbour(shifted, 1, distance)
            distance = distance * 2
    volume = 3.0 * NT * NX * NY * NZ
    return flowed, jnp.stack(entries) / volume
```

```python
import jax
import jax.numpy as jnp
from jax import lax
from jax.experimental import pallas as pl
from jax.experimental.pallas import tpu as pltpu
from jax.sharding import PartitionSpec as P

NY = 4
NZ = 32
LANES = NY * NZ
TMAX = 8
LEVELS = 5
EPS_FLOW = 0.05
TOP = 8


def product(a, b, da=False, db=False):
    out = []
    for i in range(3):
        row = []
        for j in range(3):
            rr = ii = ri = ir = None
            for k in range(3):
                ar, ai = a[k][i] if da else a[i][k]
                br, bi = b[j][k] if db else b[k][j]
                t = (ar * br, ai * bi, ar * bi, ai * br)
                if rr is None:
                    rr, ii, ri, ir = t
                else:
                    rr, ii, ri, ir = rr + t[0], ii + t[1], ri + t[2], ir + t[3]
            re = rr - ii if da == db else rr + ii
            if da and db:
                im = -(ri + ir)
            elif da:
                im = ri - ir
            elif db:
                im = ir - ri
            else:
                im = ri + ir
            row.append((re, im))
        out.append(row)
    return out


def cmul(a, b):
    return (a[0] * b[0] - a[1] * b[1], a[0] * b[1] + a[1] * b[0])


def third_row(first, second):
    out = []
    for j in range(3):
        k, l = (j + 1) % 3, (j + 2) % 3
        x, y = cmul(first[k], second[l]), cmul(first[l], second[k])
        out.append((x[0] - y[0], y[1] - x[1]))
    return out


def evolve(link, staple):
    m = product(link, staple)
    half = -0.5 * EPS_FLOW
    d = [-EPS_FLOW * m[i][i][1] for i in range(3)]
    trace = (d[0] + d[1] + d[2]) * (1.0 / 3.0)
    d = [v - trace for v in d]
    off = {}
    for i, j in ((0, 1), (0, 2), (1, 2)):
        off[i, j] = (half * (m[i][j][0] - m[j][i][0]), half * (m[i][j][1] + m[j][i][1]))
    a, b, c = off[0, 1], off[0, 2], off[1, 2]
    na, nb, nc = (v[0] * v[0] + v[1] * v[1] for v in (a, b, c))
    s = [-(d[0] * d[0] + na + nb), -(d[1] * d[1] + na + nc), -(d[2] * d[2] + nb + nc)]
    p = -0.5 * (s[0] + s[1] + s[2])

    def times_i(w, v):
        return (-w * v[1], w * v[0])

    conj = lambda v: (v[0], -v[1])
    add = lambda u, v: (u[0] + v[0], u[1] + v[1])
    sub = lambda u, v: (u[0] - v[0], u[1] - v[1])
    sq = {
        (0, 1): sub(times_i(d[0] + d[1], a), cmul(b, conj(c))),
        (0, 2): add(times_i(d[0] + d[2], b), cmul(a, c)),
        (1, 2): sub(times_i(d[1] + d[2], c), cmul(conj(a), b)),
    }
    cube = s[0] * d[0] + s[1] * d[1] + s[2] * d[2]
    for key in sq:
        u, v = sq[key], off[key]
        cube = cube - 2.0 * (u[1] * v[0] - u[0] * v[1])
    delta = cube * (1.0 / 3.0)
    e0 = (1.0 - delta * delta * (1.0 / 720.0), delta * (1.0 / 6.0 - p * (1.0 / 120.0)))
    e1 = (1.0 - p * (1.0 / 6.0 - p * (1.0 / 120.0)), delta * (1.0 / 24.0 - p * (1.0 / 360.0)))
    e2 = (0.5 - p * (1.0 / 24.0 - p * (1.0 / 720.0)), delta * (1.0 / 120.0))
    e = [[None] * 3 for _ in range(3)]
    for i in range(3):
        e[i][i] = (e0[0] - e1[1] * d[i] + e2[0] * s[i], e0[1] + e1[0] * d[i] + e2[1] * s[i])
    for i, j in off:
        e[i][j] = add(cmul(e1, off[i, j]), cmul(e2, sq[i, j]))
        x = off[i, j]
        e[j][i] = add(cmul(e1, (-x[0], x[1])), cmul(e2, conj(sq[i, j])))
    return product(e, link)


def roll(v, by, axis=1):
    by = by % v.shape[axis]
    return v if by == 0 else pltpu.roll(v, by, axis)


def shift_y(v, by):
    return roll(v, -NZ * by)


def shift_z(v, by, z):
    if by == 1:
        return jnp.where(z < NZ - 1, roll(v, -1), roll(v, NZ - 1))
    return jnp.where(z > 0, roll(v, 1), roll(v, 1 - NZ))


def flow_kernel(slices, split, links, left, right, before, after, corner_x, corner_t, out, packed, pad, sums, done, turn):
    halves = slices // 8
    end = TOP + slices

    def fill(c, _):
        for p in range(2):
            for h in range(halves):
                pad[c, 1 + p, TOP + 8 * h : TOP + 8 * h + 8, :] = links[c, pl.ds(16 * h + p, 8, stride=2), :]
            pad[c, 1 + p, TOP - 1 : TOP, :] = before[c, p : p + 1, :]
        return 0

    lax.fori_loop(0, 72, fill, 0)

    def fill_after(c, _):
        for p in range(2):
            pad[18 + c, 1 + p, end : end + 1, :] = after[c, p : p + 1, :]
        return 0

    lax.fori_loop(0, 54, fill_after, 0)

    def fill_corner(c, _):
        pad[18 + c, 0, end : end + 1, :] = corner_x[c, 0:1, :]
        pad[c, 3, TOP - 1 : TOP, :] = corner_t[c, 0:1, :]
        return 0

    lax.fori_loop(0, 18, fill_corner, 0)
    for source, plane, dirs in ((left, 0, (0, 1, 2, 3)), (right, 3, (0, 2, 3))):
        for n, d in enumerate(dirs):
            for h in range(halves):
                rows = [
                    [
                        tuple(source[12 * n + 6 * ri + 3 * i + j, 8 * h : 8 * h + 8, :] for ri in range(2))
                        for j in range(3)
                    ]
                    for i in range(2)
                ]
                rows.append(third_row(rows[0], rows[1]))
                for i in range(3):
                    for j in range(3):
                        for ri in range(2):
                            pad[18 * d + 9 * ri + 3 * i + j, plane, TOP + 8 * h : TOP + 8 * h + 8, :] = rows[i][j][ri]

    lane = lax.broadcasted_iota(jnp.int32, (8, LANES), 1)
    z = lane & (NZ - 1)

    def chunk(p, h):
        def load(d, *steps):
            dt = dx = 0
            rolls = []
            for axis, by in steps:
                if axis == 0:
                    dt += by
                elif axis == 1:
                    dx += by
                else:
                    rolls.append((axis, by))

            def one(c):
                v = pad[c, 1 + p + dx, TOP + 8 * h + dt : TOP + 8 * h + dt + 8, :]
                for axis, by in rolls:
                    v = shift_y(v, by) if axis == 2 else shift_z(v, by, z)
                return v

            return [[(one(18 * d + 3 * i + j), one(18 * d + 9 + 3 * i + j)) for j in range(3)] for i in range(3)]

        seen = set()

        def collect(d, value):
            for i in range(3):
                for j in range(3):
                    for ri in range(2):
                        at = 18 * d + 9 * ri + 3 * i + j
                        if at in seen:
                            sums[at] = sums[at] + value[i][j][ri]
                        else:
                            seen.add(at)
                            sums[at] = value[i][j][ri]

        def lower(m, v):
            if v < 2:
                q = product(load(m, (v, -1)), load(v, (m, 1), (v, -1)))
                collect(m, product(q, load(v, (v, -1)), da=True))
            else:
                q = product(product(load(m), load(v, (m, 1))), load(v), da=True)
                move = (lambda w: shift_y(w, -1)) if v == 2 else (lambda w: shift_z(w, -1, z))
                collect(m, [[(move(e[0]), move(e[1])) for e in row] for row in q])

        for m in range(4):
            for v in range(m + 1, 4):
                w = product(load(v, (m, 1)), load(m, (v, 1)), db=True)
                collect(m, product(w, load(v), db=True))
                collect(v, product(w, load(m), da=True, db=True))
                lower(m, v)
                lower(v, m)
        for m in range(4):
            staple = [
                [(sums[18 * m + 3 * i + j], sums[18 * m + 9 + 3 * i + j]) for j in range(3)] for i in range(3)
            ]
            new = evolve(load(m), staple)
            for i in range(3):
                for j in range(3):
                    for ri in range(2):
                        done[18 * m + 9 * ri + 3 * i + j, p, 8 * h : 8 * h + 8, :] = new[i][j][ri]

    def plane(p, _):
        for h in range(halves):
            chunk(p, h)
        return 0

    lax.fori_loop(0, 2, plane, 0)

    def back(c, _):
        for p in range(2):
            for h in range(halves):
                out[c, pl.ds(16 * h + p, 8, stride=2), :] = done[c, p, 8 * h : 8 * h + 8, :]
        return 0

    lax.fori_loop(0, 72, back, 0)

    width = LANES // split

    def pack(g, _):
        for p in range(2):
            for h in range(halves):
                held = [done[split * g + c, p, 8 * h : 8 * h + 8, :] for c in range(split)]
                for k in range(split):
                    mixed = None
                    for c in range(split):
                        moved = roll(held[c], width * (c - k))
                        mixed = moved if mixed is None else jnp.where(lane // width == c, moved, mixed)
                    turn[pl.ds(8 * 2 * split * h + 2 * k + p, 8, stride=2 * split), :] = mixed
        turned = jnp.transpose(turn[...])
        for c in range(split):
            packed[split * g + c] = turned[width * c : width * c + width, :]
        return 0

    lax.fori_loop(0, 36 // split, pack, 0)


def loop_kernel(blocks, per_slice, fields, out, early, lines, ahead, line_ahead):
    groups = fields.shape[2]
    lane_all = lax.broadcasted_iota(jnp.int32, (groups, LANES), 1)
    odd = (lane_all & 1) == 1
    lane = lax.broadcasted_iota(jnp.int32, (8, LANES), 1)
    slices = 16

    def forward_x(v, distance):
        if distance == 1:
            return jnp.where(odd, roll(roll(v, -1, 0), 1), roll(v, -1))
        return roll(v, -(distance // 2), 0)

    def forward_t(ref, lead, c, b, g, s):
        own = ref[lead, c, b, pl.ds(g, 8), :]
        if s == 0:
            return own
        following = ref[lead, c, lax.rem(b + 1, blocks), pl.ds(g, 8), :]
        slot = lane // per_slice if per_slice * slices == LANES else (lane // per_slice) % slices
        return roll(jnp.where(slot >= s, own, following), -per_slice * s)

    def first(b, _):
        for c in range(18):
            lines[0, c, b] = fields[18 + c, b]
            ahead[0, c, b] = forward_x(fields[c, b], 1)
        return 0

    lax.fori_loop(0, blocks, first, 0)
    for k in range(1, LEVELS):
        distance = 2 ** (k - 1)

        def grow(b, _):
            for c in range(18):
                ahead[k, c, b] = forward_x(ahead[k - 1, c, b], distance)
            own = [[(lines[k - 1, 3 * i + j, b], lines[k - 1, 9 + 3 * i + j, b]) for j in range(3)] for i in range(3)]
            far = [[tuple(forward_x(v, distance) for v in e) for e in row] for row in own]
            new = product(own, far)
            for i in range(3):
                for j in range(3):
                    for ri in range(2):
                        lines[k, 9 * ri + 3 * i + j, b] = new[i][j][ri]
            return 0

        lax.fori_loop(0, blocks, grow, 0)

    def advance(n, _):
        b = n // (groups // 8)
        g = pl.multiple_of((n % (groups // 8)) * 8, 8)
        for s in range(TMAX):
            for c in range(18):
                own = fields[c, b, pl.ds(g, 8), :]
                if s:
                    following = fields[c, lax.rem(b + 1, blocks), pl.ds(g, 8), :]
                    own = roll(jnp.where((lane // per_slice) % slices >= s, own, following), -per_slice * s)
                early[s, c, n] = own
        return 0

    cells = blocks * (groups // 8)
    lax.fori_loop(0, cells, advance, 0)

    def level(k, _):
        def cell(n, totals):
            b = n // (groups // 8)
            g = pl.multiple_of((n % (groups // 8)) * 8, 8)

            def matrix(get):
                return [[(get(3 * i + j), get(9 + 3 * i + j)) for j in range(3)] for i in range(3)]

            carried = matrix(lambda c: forward_t(lines, k, c, b, g, 0))
            new = []
            for extent in range(1, TMAX + 1):
                s = extent - 1
                carried = product(matrix(lambda c: early[s, c, n]), carried, da=True)
                carried = product(carried, matrix(lambda c: forward_t(ahead, k, c, b, g, s)))
                end = matrix(lambda c: forward_t(lines, k, c, b, g, extent))
                total = totals[s]
                for i in range(3):
                    for j in range(3):
                        total = total + (carried[i][j][0] * end[i][j][0] + carried[i][j][1] * end[i][j][1])
                new.append(total)
            return tuple(new)

        totals = lax.fori_loop(0, cells, cell, (jnp.zeros((8, LANES), jnp.float32),) * TMAX)
        for s in range(TMAX):
            out[k, pl.ds(s, 1), :] = jnp.sum(totals[s], axis=0, keepdims=True)
        return 0

    lax.fori_loop(0, LEVELS, level, 0)


def body(links):
    nta, ngx = lax.axis_size("ta"), lax.axis_size("gx")
    devices = nta * ngx
    slices = links.shape[4]
    vmem = pl.BlockSpec(memory_space=pltpu.VMEM)

    def send(value, dt, dx):
        perm = []
        for i in range(nta):
            for j in range(ngx):
                perm.append((i * ngx + j, ((i + dt) % nta) * ngx + (j + dx) % ngx))
        return lax.ppermute(value, ("ta", "gx"), perm)

    no_x = lambda v: jnp.concatenate([v[:1], v[2:]])
    left = send(links[:, :, :2, :, :, -1].reshape(48, slices, LANES), 0, 1)
    right = send(no_x(links[:, :, :2, :, :, 0]).reshape(36, slices, LANES), 0, -1)
    before = send(links[:, :, :, :, -1].reshape(72, 2, LANES), 1, 0)
    after = send(links[1:, :, :, :, 0].reshape(54, 2, LANES), -1, 0)
    corner_x = send(links[1, :, :, :, 0, -1].reshape(18, 1, LANES), -1, 1)
    corner_t = send(links[0, :, :, :, -1, 0].reshape(18, 1, LANES), 1, -1)

    split = LANES // devices
    rows = 2 * slices
    flowed, packed = pl.pallas_call(
        lambda *refs: flow_kernel(slices, split, *refs),
        out_shape=(
            jax.ShapeDtypeStruct((72, rows, LANES), jnp.float32),
            jax.ShapeDtypeStruct((36, devices, rows * split), jnp.float32),
        ),
        in_specs=[vmem] * 7,
        out_specs=(vmem, vmem),
        scratch_shapes=[
            pltpu.VMEM((72, 4, TOP + slices + 8, LANES), jnp.float32),
            pltpu.VMEM((72, 8, LANES), jnp.float32),
            pltpu.VMEM((72, 2, slices, LANES), jnp.float32),
            pltpu.VMEM((rows * split, LANES), jnp.float32),
        ],
        compiler_params=pltpu.CompilerParams(vmem_limit_bytes=40 * 2**20),
        name="flow",
    )(links.reshape(72, rows, LANES), left, right, before, after, corner_x, corner_t)

    fields = lax.all_to_all(packed, ("ta", "gx"), 1, 1, tiled=True)
    repeats = LANES // (rows * split)
    fields = fields.reshape(36, nta, ngx, rows * split)
    if repeats > 1:
        fields = jnp.tile(fields, (1, 1, 1, repeats))
    entries = pl.pallas_call(
        lambda *refs: loop_kernel(nta, 2 * split, *refs),
        out_shape=jax.ShapeDtypeStruct((LEVELS, TMAX, LANES), jnp.float32),
        in_specs=[vmem],
        out_specs=vmem,
        scratch_shapes=[
            pltpu.VMEM((TMAX, 18, nta * (ngx // 8), 8, LANES), jnp.float32),
            pltpu.VMEM((LEVELS, 18, nta, ngx, LANES), jnp.float32),
            pltpu.VMEM((LEVELS, 18, nta, ngx, LANES), jnp.float32),
            pltpu.VMEM((8, LANES), jnp.float32),
        ],
        compiler_params=pltpu.CompilerParams(vmem_limit_bytes=40 * 2**20),
        name="loops",
    )(fields)
    volume = 3.0 * slices * nta * 2 * ngx * LANES
    table = lax.psum(jnp.sum(entries, axis=2), ("ta", "gx")) / (volume * repeats)
    return flowed.reshape(links.shape), table


def solution(mesh):
    spec = P(None, None, None, None, "ta", "gx", None)
    return jax.shard_map(body, mesh=mesh, in_specs=(spec,), out_specs=(spec, P()), check_vma=False)
```

```python
import jax
import jax.numpy as jnp
from jax import lax
from jax.experimental import pallas as pl
from jax.experimental.pallas import tpu as pltpu
from jax.sharding import PartitionSpec as P

NY = 4
NZ = 32
LANES = NY * NZ
TMAX = 8
LEVELS = 5
EPS_FLOW = 0.05
TOP = 8


def product(a, b, da=False, db=False):
    out = []
    for i in range(3):
        row = []
        for j in range(3):
            rr = ii = ri = ir = None
            for k in range(3):
                ar, ai = a[k][i] if da else a[i][k]
                br, bi = b[j][k] if db else b[k][j]
                t = (ar * br, ai * bi, ar * bi, ai * br)
                if rr is None:
                    rr, ii, ri, ir = t
                else:
                    rr, ii, ri, ir = rr + t[0], ii + t[1], ri + t[2], ir + t[3]
            re = rr - ii if da == db else rr + ii
            if da and db:
                im = -(ri + ir)
            elif da:
                im = ri - ir
            elif db:
                im = ir - ri
            else:
                im = ri + ir
            row.append((re, im))
        out.append(row)
    return out


def cmul(a, b):
    return (a[0] * b[0] - a[1] * b[1], a[0] * b[1] + a[1] * b[0])


def third_row(first, second):
    out = []
    for j in range(3):
        k, l = (j + 1) % 3, (j + 2) % 3
        x, y = cmul(first[k], second[l]), cmul(first[l], second[k])
        out.append((x[0] - y[0], y[1] - x[1]))
    return out


def evolve(link, staple):
    m = product(link, staple)
    half = -0.5 * EPS_FLOW
    d = [-EPS_FLOW * m[i][i][1] for i in range(3)]
    trace = (d[0] + d[1] + d[2]) * (1.0 / 3.0)
    d = [v - trace for v in d]
    off = {}
    for i, j in ((0, 1), (0, 2), (1, 2)):
        off[i, j] = (half * (m[i][j][0] - m[j][i][0]), half * (m[i][j][1] + m[j][i][1]))
    a, b, c = off[0, 1], off[0, 2], off[1, 2]
    na, nb, nc = (v[0] * v[0] + v[1] * v[1] for v in (a, b, c))
    s = [-(d[0] * d[0] + na + nb), -(d[1] * d[1] + na + nc), -(d[2] * d[2] + nb + nc)]
    p = -0.5 * (s[0] + s[1] + s[2])

    def times_i(w, v):
        return (-w * v[1], w * v[0])

    conj = lambda v: (v[0], -v[1])
    add = lambda u, v: (u[0] + v[0], u[1] + v[1])
    sub = lambda u, v: (u[0] - v[0], u[1] - v[1])
    sq = {
        (0, 1): sub(times_i(d[0] + d[1], a), cmul(b, conj(c))),
        (0, 2): add(times_i(d[0] + d[2], b), cmul(a, c)),
        (1, 2): sub(times_i(d[1] + d[2], c), cmul(conj(a), b)),
    }
    cube = s[0] * d[0] + s[1] * d[1] + s[2] * d[2]
    for key in sq:
        u, v = sq[key], off[key]
        cube = cube - 2.0 * (u[1] * v[0] - u[0] * v[1])
    delta = cube * (1.0 / 3.0)
    e0 = (1.0 - delta * delta * (1.0 / 720.0), delta * (1.0 / 6.0 - p * (1.0 / 120.0)))
    e1 = (1.0 - p * (1.0 / 6.0 - p * (1.0 / 120.0)), delta * (1.0 / 24.0 - p * (1.0 / 360.0)))
    e2 = (0.5 - p * (1.0 / 24.0 - p * (1.0 / 720.0)), delta * (1.0 / 120.0))
    e = [[None] * 3 for _ in range(3)]
    for i in range(3):
        e[i][i] = (e0[0] - e1[1] * d[i] + e2[0] * s[i], e0[1] + e1[0] * d[i] + e2[1] * s[i])
    for i, j in off:
        e[i][j] = add(cmul(e1, off[i, j]), cmul(e2, sq[i, j]))
        x = off[i, j]
        e[j][i] = add(cmul(e1, (-x[0], x[1])), cmul(e2, conj(sq[i, j])))
    return product(e, link)


def roll(v, by, axis=1):
    by = by % v.shape[axis]
    return v if by == 0 else pltpu.roll(v, by, axis)


def shift_y(v, by):
    return roll(v, -NZ * by)


def shift_z(v, by, z):
    if by == 1:
        return jnp.where(z < NZ - 1, roll(v, -1), roll(v, NZ - 1))
    return jnp.where(z > 0, roll(v, 1), roll(v, 1 - NZ))


def flow_kernel(slices, split, links, left, right, before, after, corner_x, corner_t, out, packed, pad, sums, done, turn):
    halves = slices // 8
    end = TOP + slices

    def fill(c, _):
        for p in range(2):
            for h in range(halves):
                pad[c, 1 + p, TOP + 8 * h : TOP + 8 * h + 8, :] = links[c, pl.ds(16 * h + p, 8, stride=2), :]
            pad[c, 1 + p, TOP - 1 : TOP, :] = before[c, p : p + 1, :]
        return 0

    lax.fori_loop(0, 72, fill, 0)

    def fill_after(c, _):
        for p in range(2):
            pad[18 + c, 1 + p, end : end + 1, :] = after[c, p : p + 1, :]
        return 0

    lax.fori_loop(0, 54, fill_after, 0)

    def fill_corner(c, _):
        pad[18 + c, 0, end : end + 1, :] = corner_x[c, 0:1, :]
        pad[c, 3, TOP - 1 : TOP, :] = corner_t[c, 0:1, :]
        return 0

    lax.fori_loop(0, 18, fill_corner, 0)
    for source, plane, dirs in ((left, 0, (0, 1, 2, 3)), (right, 3, (0, 2, 3))):
        for n, d in enumerate(dirs):
            for h in range(halves):
                rows = [
                    [
                        tuple(source[12 * n + 6 * ri + 3 * i + j, 8 * h : 8 * h + 8, :] for ri in range(2))
                        for j in range(3)
                    ]
                    for i in range(2)
                ]
                rows.append(third_row(rows[0], rows[1]))
                for i in range(3):
                    for j in range(3):
                        for ri in range(2):
                            pad[18 * d + 9 * ri + 3 * i + j, plane, TOP + 8 * h : TOP + 8 * h + 8, :] = rows[i][j][ri]

    lane = lax.broadcasted_iota(jnp.int32, (8, LANES), 1)
    z = lane & (NZ - 1)

    def chunk(p, h):
        def load(d, *steps):
            dt = dx = 0
            rolls = []
            for axis, by in steps:
                if axis == 0:
                    dt += by
                elif axis == 1:
                    dx += by
                else:
                    rolls.append((axis, by))

            def one(c):
                v = pad[c, 1 + p + dx, TOP + 8 * h + dt : TOP + 8 * h + dt + 8, :]
                for axis, by in rolls:
                    v = shift_y(v, by) if axis == 2 else shift_z(v, by, z)
                return v

            return [[(one(18 * d + 3 * i + j), one(18 * d + 9 + 3 * i + j)) for j in range(3)] for i in range(3)]

        seen = set()

        def collect(d, value):
            for i in range(3):
                for j in range(3):
                    for ri in range(2):
                        at = 18 * d + 9 * ri + 3 * i + j
                        if at in seen:
                            sums[at] = sums[at] + value[i][j][ri]
                        else:
                            seen.add(at)
                            sums[at] = value[i][j][ri]

        def lower(m, v):
            if v < 2:
                q = product(load(m, (v, -1)), load(v, (m, 1), (v, -1)))
                collect(m, product(q, load(v, (v, -1)), da=True))
            else:
                q = product(product(load(m), load(v, (m, 1))), load(v), da=True)
                move = (lambda w: shift_y(w, -1)) if v == 2 else (lambda w: shift_z(w, -1, z))
                collect(m, [[(move(e[0]), move(e[1])) for e in row] for row in q])

        for m in range(4):
            for v in range(m + 1, 4):
                w = product(load(v, (m, 1)), load(m, (v, 1)), db=True)
                collect(m, product(w, load(v), db=True))
                collect(v, product(w, load(m), da=True, db=True))
                lower(m, v)
                lower(v, m)
        for m in range(4):
            staple = [
                [(sums[18 * m + 3 * i + j], sums[18 * m + 9 + 3 * i + j]) for j in range(3)] for i in range(3)
            ]
            new = evolve(load(m), staple)
            for i in range(3):
                for j in range(3):
                    for ri in range(2):
                        done[18 * m + 9 * ri + 3 * i + j, p, 8 * h : 8 * h + 8, :] = new[i][j][ri]

    def plane(p, _):
        for h in range(halves):
            chunk(p, h)
        return 0

    lax.fori_loop(0, 2, plane, 0)

    def back(c, _):
        for p in range(2):
            for h in range(halves):
                out[c, pl.ds(16 * h + p, 8, stride=2), :] = done[c, p, 8 * h : 8 * h + 8, :]
        return 0

    lax.fori_loop(0, 72, back, 0)

    width = LANES // split

    def pack(g, _):
        for p in range(2):
            for h in range(halves):
                held = [done[split * g + c, p, 8 * h : 8 * h + 8, :] for c in range(split)]
                for k in range(split):
                    mixed = None
                    for c in range(split):
                        moved = roll(held[c], width * (c - k))
                        mixed = moved if mixed is None else jnp.where(lane // width == c, moved, mixed)
                    turn[pl.ds(8 * 2 * split * h + 2 * k + p, 8, stride=2 * split), :] = mixed
        turned = jnp.transpose(turn[...])
        for c in range(split):
            packed[split * g + c] = turned[width * c : width * c + width, :]
        return 0

    lax.fori_loop(0, 36 // split, pack, 0)


def loop_kernel(blocks, per_slice, fields, out, early, lines, ahead):
    groups = fields.shape[2]
    lane_all = lax.broadcasted_iota(jnp.int32, (groups, LANES), 1)
    odd = (lane_all & 1) == 1
    lane = lax.broadcasted_iota(jnp.int32, (8, LANES), 1)
    slices = 16

    def forward_x(v, distance):
        if distance == 1:
            return jnp.where(odd, roll(roll(v, -1, 0), 1), roll(v, -1))
        return roll(v, -(distance // 2), 0)

    def forward_t(ref, lead, c, b, g, s):
        own = ref[lead, c, b, pl.ds(g, 8), :]
        if s == 0:
            return own
        following = ref[lead, c, lax.rem(b + 1, blocks), pl.ds(g, 8), :]
        slot = lane // per_slice if per_slice * slices == LANES else (lane // per_slice) % slices
        return roll(jnp.where(slot >= s, own, following), -per_slice * s)

    def first(b, _):
        for c in range(18):
            lines[0, c, b] = fields[18 + c, b]
            ahead[0, c, b] = forward_x(fields[c, b], 1)
        return 0

    lax.fori_loop(0, blocks, first, 0)
    for k in range(1, LEVELS):
        distance = 2 ** (k - 1)

        def grow(b, _):
            for c in range(18):
                ahead[k, c, b] = forward_x(ahead[k - 1, c, b], distance)
            own = [[(lines[k - 1, 3 * i + j, b], lines[k - 1, 9 + 3 * i + j, b]) for j in range(3)] for i in range(3)]
            far = [[tuple(forward_x(v, distance) for v in e) for e in row] for row in own]
            new = product(own, far)
            for i in range(3):
                for j in range(3):
                    for ri in range(2):
                        lines[k, 9 * ri + 3 * i + j, b] = new[i][j][ri]
            return 0

        lax.fori_loop(0, blocks, grow, 0)

    def advance(n, _):
        b = n // (groups // 8)
        g = pl.multiple_of((n % (groups // 8)) * 8, 8)
        for s in range(TMAX):
            for c in range(18):
                own = fields[c, b, pl.ds(g, 8), :]
                if s:
                    following = fields[c, lax.rem(b + 1, blocks), pl.ds(g, 8), :]
                    own = roll(jnp.where((lane // per_slice) % slices >= s, own, following), -per_slice * s)
                early[s, c, n] = own
        return 0

    cells = blocks * (groups // 8)
    lax.fori_loop(0, cells, advance, 0)

    def level(k, _):
        def cell(n, totals):
            b = n // (groups // 8)
            g = pl.multiple_of((n % (groups // 8)) * 8, 8)

            def matrix(get):
                return [[(get(3 * i + j), get(9 + 3 * i + j)) for j in range(3)] for i in range(3)]

            carried = matrix(lambda c: forward_t(lines, k, c, b, g, 0))
            new = []
            for extent in range(1, TMAX + 1):
                s = extent - 1
                carried = product(matrix(lambda c: early[s, c, n]), carried, da=True)
                carried = product(carried, matrix(lambda c: forward_t(ahead, k, c, b, g, s)))
                end = matrix(lambda c: forward_t(lines, k, c, b, g, extent))
                total = totals[s]
                for i in range(3):
                    for j in range(3):
                        total = total + (carried[i][j][0] * end[i][j][0] + carried[i][j][1] * end[i][j][1])
                new.append(total)
            return tuple(new)

        totals = lax.fori_loop(0, cells, cell, (jnp.zeros((8, LANES), jnp.float32),) * TMAX)
        block = jnp.concatenate([jnp.sum(t, axis=0, keepdims=True) for t in totals], axis=0)
        out[...] = jnp.where(lane == k, jnp.sum(block, axis=1, keepdims=True), out[...])
        return 0

    out[...] = jnp.zeros((TMAX, LANES), jnp.float32)
    lax.fori_loop(0, LEVELS, level, 0)


MESH = pl.DeviceIdType.MESH


def halo_kernel(nta, ngx, slices, links, left, right, before, after, corner_x, corner_t, send_sems, recv_sems):
    ta, gx = lax.axis_index("ta"), lax.axis_index("gx")
    there = lambda dt, dx: (lax.rem(ta + dt + nta, nta), lax.rem(gx + dx + ngx, ngx))
    barrier = pltpu.get_barrier_semaphore()
    steps = ((0, 1), (0, -1), (1, 0), (-1, 0), (-1, 1), (1, -1))
    for step in steps:
        pl.semaphore_signal(barrier, inc=1, device_id=there(*step), device_id_type=MESH)
    pl.semaphore_wait(barrier, len(steps))
    last = slices - 1
    moves = (
        (links.at[:, 0:6, :, 1], left, (0, 1)),
        (links.at[0:2, 0:6, :, 0], right.at[0:2], (0, -1)),
        (links.at[4:8, 0:6, :, 0], right.at[2:6], (0, -1)),
        (links.at[:, :, last], before, (1, 0)),
        (links.at[2:8, :, 0], after, (-1, 0)),
        (links.at[2:4, :, 0, 1], corner_x, (-1, 1)),
        (links.at[0:2, :, last, 0], corner_t, (1, -1)),
    )
    copies = [
        pltpu.make_async_remote_copy(
            src_ref=source,
            dst_ref=target,
            send_sem=send_sems.at[n],
            recv_sem=recv_sems.at[n],
            device_id=there(*step),
            device_id_type=MESH,
        )
        for n, (source, target, step) in enumerate(moves)
    ]
    for copy in copies:
        copy.start()
    for copy in copies:
        copy.wait()


def meet_all(ngx, devices, me):
    barrier = pltpu.get_barrier_semaphore()

    def greet(k, _):
        other = lax.rem(me + k, devices)
        pl.semaphore_signal(barrier, inc=1, device_id=(other // ngx, lax.rem(other, ngx)), device_id_type=MESH)
        return 0

    lax.fori_loop(1, devices, greet, 0)
    pl.semaphore_wait(barrier, devices - 1)


def exchange_kernel(nta, ngx, packed, fields, send_sems, recv_sems, own_sem):
    devices = nta * ngx
    me = lax.axis_index("ta") * ngx + lax.axis_index("gx")
    meet_all(ngx, devices, me)

    def move(k):
        other = lax.rem(me + k, devices)
        return pltpu.make_async_remote_copy(
            src_ref=packed.at[:, other],
            dst_ref=fields.at[:, me],
            send_sem=send_sems.at[k],
            recv_sem=recv_sems.at[k],
            device_id=(other // ngx, lax.rem(other, ngx)),
            device_id_type=MESH,
        )

    def start(k, _):
        move(k).start()
        return 0

    def wait(k, _):
        move(k).wait()
        return 0

    lax.fori_loop(1, devices, start, 0)
    own = pltpu.make_async_copy(packed.at[:, me], fields.at[:, me], own_sem)
    own.start()
    own.wait()
    lax.fori_loop(1, devices, wait, 0)


def total_kernel(nta, ngx, scale, part, total, slots, send_sems, recv_sems):
    devices = nta * ngx
    me = lax.axis_index("ta") * ngx + lax.axis_index("gx")
    meet_all(ngx, devices, me)

    def move(k):
        other = lax.rem(me + k, devices)
        return pltpu.make_async_remote_copy(
            src_ref=part,
            dst_ref=slots.at[me],
            send_sem=send_sems.at[k],
            recv_sem=recv_sems.at[k],
            device_id=(other // ngx, lax.rem(other, ngx)),
            device_id_type=MESH,
        )

    def start(k, _):
        move(k).start()
        return 0

    def wait(k, _):
        move(k).wait()
        return 0

    lax.fori_loop(1, devices, start, 0)
    slots[me] = part[...]
    lax.fori_loop(1, devices, wait, 0)
    total[...] = jnp.sum(slots[...], axis=0) * scale


def body(links):
    nta, ngx = lax.axis_size("ta"), lax.axis_size("gx")
    devices = nta * ngx
    slices = links.shape[4]
    vmem = pl.BlockSpec(memory_space=pltpu.VMEM)
    anywhere = pl.BlockSpec(memory_space=pl.ANY)
    array = lambda *shape: jax.ShapeDtypeStruct(shape, jnp.float32)
    sems = pltpu.SemaphoreType.DMA
    remote = lambda n: pltpu.CompilerParams(collective_id=n, has_side_effects=True)

    halos = pl.pallas_call(
        lambda *refs: halo_kernel(nta, ngx, slices, *refs),
        out_shape=(
            array(8, 6, slices, 1, LANES),
            array(6, 6, slices, 1, LANES),
            array(8, 9, 2, 1, LANES),
            array(6, 9, 2, 1, LANES),
            array(2, 9, 1, LANES),
            array(2, 9, 1, LANES),
        ),
        in_specs=[anywhere],
        out_specs=(vmem,) * 6,
        scratch_shapes=[sems((7,)), sems((7,))],
        compiler_params=remote(0),
        name="halos",
    )(links.reshape(8, 9, slices, 2, 1, LANES))
    shapes = ((48, slices, LANES), (36, slices, LANES), (72, 2, LANES), (54, 2, LANES), (18, 1, LANES), (18, 1, LANES))
    halos = [v.reshape(shape) for v, shape in zip(halos, shapes)]

    split = LANES // devices
    rows = 2 * slices
    width = rows * split
    flowed, packed = pl.pallas_call(
        lambda *refs: flow_kernel(slices, split, *refs),
        out_shape=(array(72, rows, LANES), array(36, devices, width)),
        in_specs=[vmem] * 7,
        out_specs=(vmem, vmem),
        scratch_shapes=[
            pltpu.VMEM((72, 4, TOP + slices + 8, LANES), jnp.float32),
            pltpu.VMEM((72, 8, LANES), jnp.float32),
            pltpu.VMEM((72, 2, slices, LANES), jnp.float32),
            pltpu.VMEM((width, LANES), jnp.float32),
        ],
        compiler_params=pltpu.CompilerParams(vmem_limit_bytes=40 * 2**20),
        name="flow",
    )(links.reshape(72, rows, LANES), *halos)

    fields = pl.pallas_call(
        lambda *refs: exchange_kernel(nta, ngx, *refs),
        out_shape=array(36, devices, 1, width),
        in_specs=[vmem],
        out_specs=vmem,
        scratch_shapes=[sems((devices,)), sems((devices,)), sems],
        compiler_params=remote(1),
        name="exchange",
    )(packed.reshape(36, devices, 1, width))
    repeats = LANES // width
    fields = fields.reshape(36, nta, ngx, width)
    if repeats > 1:
        fields = jnp.tile(fields, (1, 1, 1, repeats))
    part = pl.pallas_call(
        lambda *refs: loop_kernel(nta, 2 * split, *refs),
        out_shape=array(TMAX, LANES),
        in_specs=[vmem],
        out_specs=vmem,
        scratch_shapes=[
            pltpu.VMEM((TMAX, 18, nta * (ngx // 8), 8, LANES), jnp.float32),
            pltpu.VMEM((LEVELS, 18, nta, ngx, LANES), jnp.float32),
            pltpu.VMEM((LEVELS, 18, nta, ngx, LANES), jnp.float32),
        ],
        compiler_params=pltpu.CompilerParams(vmem_limit_bytes=40 * 2**20),
        name="loops",
    )(fields)
    scale = 1.0 / (3.0 * slices * nta * 2 * ngx * LANES * repeats)
    total = pl.pallas_call(
        lambda *refs: total_kernel(nta, ngx, scale, *refs),
        out_shape=array(TMAX, LANES),
        in_specs=[vmem],
        out_specs=vmem,
        scratch_shapes=[pltpu.VMEM((devices, TMAX, LANES), jnp.float32), sems((devices,)), sems((devices,))],
        compiler_params=remote(2),
        name="total",
    )(part)
    return flowed.reshape(links.shape), total[:, :LEVELS].T


def solution(mesh):
    spec = P(None, None, None, None, "ta", "gx", None)
    return jax.shard_map(body, mesh=mesh, in_specs=(spec,), out_specs=(spec, P()), check_vma=False)
```

```python
import jax
import jax.numpy as jnp
from jax import lax
from jax.experimental import pallas as pl
from jax.experimental.pallas import tpu as pltpu
from jax.sharding import PartitionSpec as P

NY = 4
NZ = 32
LANES = NY * NZ
TMAX = 8
LEVELS = 5
EPS_FLOW = 0.05
TOP = 8


def product(a, b, da=False, db=False):
    out = []
    for i in range(3):
        row = []
        for j in range(3):
            rr = ii = ri = ir = None
            for k in range(3):
                ar, ai = a[k][i] if da else a[i][k]
                br, bi = b[j][k] if db else b[k][j]
                t = (ar * br, ai * bi, ar * bi, ai * br)
                if rr is None:
                    rr, ii, ri, ir = t
                else:
                    rr, ii, ri, ir = rr + t[0], ii + t[1], ri + t[2], ir + t[3]
            re = rr - ii if da == db else rr + ii
            if da and db:
                im = -(ri + ir)
            elif da:
                im = ri - ir
            elif db:
                im = ir - ri
            else:
                im = ri + ir
            row.append((re, im))
        out.append(row)
    return out


def cmul(a, b):
    return (a[0] * b[0] - a[1] * b[1], a[0] * b[1] + a[1] * b[0])


def third_row(first, second):
    out = []
    for j in range(3):
        k, l = (j + 1) % 3, (j + 2) % 3
        x, y = cmul(first[k], second[l]), cmul(first[l], second[k])
        out.append((x[0] - y[0], y[1] - x[1]))
    return out


def evolve(link, staple):
    m = product(link, staple)
    half = -0.5 * EPS_FLOW
    d = [-EPS_FLOW * m[i][i][1] for i in range(3)]
    trace = (d[0] + d[1] + d[2]) * (1.0 / 3.0)
    d = [v - trace for v in d]
    off = {}
    for i, j in ((0, 1), (0, 2), (1, 2)):
        off[i, j] = (half * (m[i][j][0] - m[j][i][0]), half * (m[i][j][1] + m[j][i][1]))
    a, b, c = off[0, 1], off[0, 2], off[1, 2]
    na, nb, nc = (v[0] * v[0] + v[1] * v[1] for v in (a, b, c))
    s = [-(d[0] * d[0] + na + nb), -(d[1] * d[1] + na + nc), -(d[2] * d[2] + nb + nc)]
    p = -0.5 * (s[0] + s[1] + s[2])

    def times_i(w, v):
        return (-w * v[1], w * v[0])

    conj = lambda v: (v[0], -v[1])
    add = lambda u, v: (u[0] + v[0], u[1] + v[1])
    sub = lambda u, v: (u[0] - v[0], u[1] - v[1])
    sq = {
        (0, 1): sub(times_i(d[0] + d[1], a), cmul(b, conj(c))),
        (0, 2): add(times_i(d[0] + d[2], b), cmul(a, c)),
        (1, 2): sub(times_i(d[1] + d[2], c), cmul(conj(a), b)),
    }
    cube = s[0] * d[0] + s[1] * d[1] + s[2] * d[2]
    for key in sq:
        u, v = sq[key], off[key]
        cube = cube - 2.0 * (u[1] * v[0] - u[0] * v[1])
    delta = cube * (1.0 / 3.0)
    e0 = (1.0 - delta * delta * (1.0 / 720.0), delta * (1.0 / 6.0 - p * (1.0 / 120.0)))
    e1 = (1.0 - p * (1.0 / 6.0 - p * (1.0 / 120.0)), delta * (1.0 / 24.0 - p * (1.0 / 360.0)))
    e2 = (0.5 - p * (1.0 / 24.0 - p * (1.0 / 720.0)), delta * (1.0 / 120.0))
    e = [[None] * 3 for _ in range(3)]
    for i in range(3):
        e[i][i] = (e0[0] - e1[1] * d[i] + e2[0] * s[i], e0[1] + e1[0] * d[i] + e2[1] * s[i])
    for i, j in off:
        e[i][j] = add(cmul(e1, off[i, j]), cmul(e2, sq[i, j]))
        x = off[i, j]
        e[j][i] = add(cmul(e1, (-x[0], x[1])), cmul(e2, conj(sq[i, j])))
    return product(e, link)


def roll(v, by, axis=1):
    by = by % v.shape[axis]
    return v if by == 0 else pltpu.roll(v, by, axis)


def shift_y(v, by):
    return roll(v, -NZ * by)


def shift_z(v, by, z):
    if by == 1:
        return jnp.where(z < NZ - 1, roll(v, -1), roll(v, NZ - 1))
    return jnp.where(z > 0, roll(v, 1), roll(v, 1 - NZ))


def flow_kernel(slices, split, links, left, right, before, after, corner_x, corner_t, out, packed, pad, sums, done, turn):
    halves = slices // 8
    end = TOP + slices

    def fill(c, _):
        for p in range(2):
            for h in range(halves):
                pad[c, 1 + p, TOP + 8 * h : TOP + 8 * h + 8, :] = links[c, pl.ds(16 * h + p, 8, stride=2), :]
            pad[c, 1 + p, TOP - 1 : TOP, :] = before[c, p : p + 1, :]
        return 0

    lax.fori_loop(0, 72, fill, 0)

    def fill_after(c, _):
        for p in range(2):
            pad[18 + c, 1 + p, end : end + 1, :] = after[c, p : p + 1, :]
        return 0

    lax.fori_loop(0, 54, fill_after, 0)

    def fill_corner(c, _):
        pad[18 + c, 0, end : end + 1, :] = corner_x[c, 0:1, :]
        pad[c, 3, TOP - 1 : TOP, :] = corner_t[c, 0:1, :]
        return 0

    lax.fori_loop(0, 18, fill_corner, 0)
    for source, plane, dirs in ((left, 0, (0, 1, 2, 3)), (right, 3, (0, 2, 3))):
        for n, d in enumerate(dirs):
            for h in range(halves):
                rows = [
                    [
                        tuple(source[12 * n + 6 * ri + 3 * i + j, 8 * h : 8 * h + 8, :] for ri in range(2))
                        for j in range(3)
                    ]
                    for i in range(2)
                ]
                rows.append(third_row(rows[0], rows[1]))
                for i in range(3):
                    for j in range(3):
                        for ri in range(2):
                            pad[18 * d + 9 * ri + 3 * i + j, plane, TOP + 8 * h : TOP + 8 * h + 8, :] = rows[i][j][ri]

    lane = lax.broadcasted_iota(jnp.int32, (8, LANES), 1)
    z = lane & (NZ - 1)

    def chunk(p, h):
        def load(d, *steps):
            dt = dx = 0
            rolls = []
            for axis, by in steps:
                if axis == 0:
                    dt += by
                elif axis == 1:
                    dx += by
                else:
                    rolls.append((axis, by))

            def one(c):
                v = pad[c, 1 + p + dx, TOP + 8 * h + dt : TOP + 8 * h + dt + 8, :]
                for axis, by in rolls:
                    v = shift_y(v, by) if axis == 2 else shift_z(v, by, z)
                return v

            return [[(one(18 * d + 3 * i + j), one(18 * d + 9 + 3 * i + j)) for j in range(3)] for i in range(3)]

        seen = set()

        def collect(d, value):
            for i in range(3):
                for j in range(3):
                    for ri in range(2):
                        at = 18 * d + 9 * ri + 3 * i + j
                        if at in seen:
                            sums[at] = sums[at] + value[i][j][ri]
                        else:
                            seen.add(at)
                            sums[at] = value[i][j][ri]

        def lower(m, v):
            if v < 2:
                q = product(load(m, (v, -1)), load(v, (m, 1), (v, -1)))
                collect(m, product(q, load(v, (v, -1)), da=True))
            else:
                q = product(product(load(m), load(v, (m, 1))), load(v), da=True)
                move = (lambda w: shift_y(w, -1)) if v == 2 else (lambda w: shift_z(w, -1, z))
                collect(m, [[(move(e[0]), move(e[1])) for e in row] for row in q])

        for m in range(4):
            for v in range(m + 1, 4):
                w = product(load(v, (m, 1)), load(m, (v, 1)), db=True)
                collect(m, product(w, load(v), db=True))
                collect(v, product(w, load(m), da=True, db=True))
                lower(m, v)
                lower(v, m)
        for m in range(4):
            staple = [
                [(sums[18 * m + 3 * i + j], sums[18 * m + 9 + 3 * i + j]) for j in range(3)] for i in range(3)
            ]
            new = evolve(load(m), staple)
            for i in range(3):
                for j in range(3):
                    for ri in range(2):
                        done[18 * m + 9 * ri + 3 * i + j, p, 8 * h : 8 * h + 8, :] = new[i][j][ri]

    def plane(p, _):
        for h in range(halves):
            chunk(p, h)
        return 0

    lax.fori_loop(0, 2, plane, 0)

    def back(c, _):
        for p in range(2):
            for h in range(halves):
                out[c, pl.ds(16 * h + p, 8, stride=2), :] = done[c, p, 8 * h : 8 * h + 8, :]
        return 0

    lax.fori_loop(0, 72, back, 0)

    width = LANES // split

    def pack(g, _):
        for p in range(2):
            for h in range(halves):
                held = [done[split * g + c, p, 8 * h : 8 * h + 8, :] for c in range(split)]
                for k in range(split):
                    mixed = None
                    for c in range(split):
                        moved = roll(held[c], width * (c - k))
                        mixed = moved if mixed is None else jnp.where(lane // width == c, moved, mixed)
                    turn[pl.ds(8 * 2 * split * h + 2 * k + p, 8, stride=2 * split), :] = mixed
        turned = jnp.transpose(turn[...])
        for c in range(split):
            packed[pl.ds(split * g + c, width, stride=36), :] = turned[width * c : width * c + width, :]
        return 0

    for g in range(36 // split):
        pack(g, 0)


def loop_kernel(blocks, per_slice, arrived, out, fields, early, lines, ahead):
    groups = fields.shape[2]
    for b in range(blocks):
        for c in range(36):
            fields[c, b] = arrived[pl.ds(36 * groups * b + c, groups, stride=36), :]
    lane_all = lax.broadcasted_iota(jnp.int32, (groups, LANES), 1)
    odd = (lane_all & 1) == 1
    lane = lax.broadcasted_iota(jnp.int32, (8, LANES), 1)
    row = lax.broadcasted_iota(jnp.int32, (8, LANES), 0)
    slices = 16

    def forward_x(v, distance):
        if distance == 1:
            return jnp.where(odd, roll(roll(v, -1, 0), 1), roll(v, -1))
        return roll(v, -(distance // 2), 0)

    def forward_t(ref, lead, c, b, g, s):
        own = ref[lead, c, b, pl.ds(g, 8), :]
        if s == 0:
            return own
        following = ref[lead, c, lax.rem(b + 1, blocks), pl.ds(g, 8), :]
        slot = lane // per_slice if per_slice * slices == LANES else (lane // per_slice) % slices
        return roll(jnp.where(slot >= s, own, following), -per_slice * s)

    def first(b, _):
        for c in range(18):
            lines[0, c, b] = fields[18 + c, b]
            ahead[0, c, b] = forward_x(fields[c, b], 1)
        return 0

    lax.fori_loop(0, blocks, first, 0)
    for k in range(1, LEVELS):
        distance = 2 ** (k - 1)

        def grow(b, _):
            for c in range(18):
                ahead[k, c, b] = forward_x(ahead[k - 1, c, b], distance)
            own = [[(lines[k - 1, 3 * i + j, b], lines[k - 1, 9 + 3 * i + j, b]) for j in range(3)] for i in range(3)]
            far = [[tuple(forward_x(v, distance) for v in e) for e in row] for row in own]
            new = product(own, far)
            for i in range(3):
                for j in range(3):
                    for ri in range(2):
                        lines[k, 9 * ri + 3 * i + j, b] = new[i][j][ri]
            return 0

        lax.fori_loop(0, blocks, grow, 0)

    def advance(n, _):
        b = n // (groups // 8)
        g = pl.multiple_of((n % (groups // 8)) * 8, 8)
        for s in range(TMAX):
            for c in range(18):
                own = fields[c, b, pl.ds(g, 8), :]
                if s:
                    following = fields[c, lax.rem(b + 1, blocks), pl.ds(g, 8), :]
                    own = roll(jnp.where((lane // per_slice) % slices >= s, own, following), -per_slice * s)
                early[s, c, n] = own
        return 0

    cells = blocks * (groups // 8)
    lax.fori_loop(0, cells, advance, 0)

    def level(k, _):
        def cell(n, totals):
            b = n // (groups // 8)
            g = pl.multiple_of((n % (groups // 8)) * 8, 8)

            def matrix(get):
                return [[(get(3 * i + j), get(9 + 3 * i + j)) for j in range(3)] for i in range(3)]

            carried = matrix(lambda c: forward_t(lines, k, c, b, g, 0))
            new = []
            for extent in range(1, TMAX + 1):
                s = extent - 1
                carried = product(matrix(lambda c: early[s, c, n]), carried, da=True)
                carried = product(carried, matrix(lambda c: forward_t(ahead, k, c, b, g, s)))
                end = matrix(lambda c: forward_t(lines, k, c, b, g, extent))
                total = totals[s]
                for i in range(3):
                    for j in range(3):
                        total = total + (carried[i][j][0] * end[i][j][0] + carried[i][j][1] * end[i][j][1])
                new.append(total)
            return tuple(new)

        totals = lax.fori_loop(0, cells, cell, (jnp.zeros((8, LANES), jnp.float32),) * TMAX)
        block = jnp.concatenate([jnp.sum(t, axis=0, keepdims=True) for t in totals], axis=0)
        spread = jnp.where(lane == row, jnp.sum(block, axis=1, keepdims=True), 0.0)
        out[...] = jnp.where(row == k, jnp.sum(spread, axis=0, keepdims=True), out[...])
        return 0

    out[...] = jnp.zeros((TMAX, LANES), jnp.float32)
    lax.fori_loop(0, LEVELS, level, 0)


MESH = pl.DeviceIdType.MESH


def halo_kernel(nta, ngx, slices, links, left, right, before, after, corner_x, corner_t, last_plane, first_plane, local_sems, send_sems, recv_sems):
    ta, gx = lax.axis_index("ta"), lax.axis_index("gx")
    there = lambda dt, dx: (lax.rem(ta + dt + nta, nta), lax.rem(gx + dx + ngx, ngx))
    local = [
        pltpu.make_async_copy(source, target, local_sems.at[n])
        for n, (source, target) in enumerate(
            (
                (links.at[:, 0:6, :, 1], last_plane),
                (links.at[0:2, 0:6, :, 0], first_plane.at[0:2]),
                (links.at[4:8, 0:6, :, 0], first_plane.at[2:6]),
            )
        )
    ]
    for copy in local:
        copy.start()
    barrier = pltpu.get_barrier_semaphore()
    steps = ((0, 1), (0, -1), (1, 0), (-1, 0), (-1, 1), (1, -1))
    for step in steps:
        pl.semaphore_signal(barrier, inc=1, device_id=there(*step), device_id_type=MESH)
    pl.semaphore_wait(barrier, len(steps))
    last = slices - 1
    for copy in local:
        copy.wait()
    moves = (
        (last_plane, left, (0, 1)),
        (first_plane, right, (0, -1)),
        (links.at[:, :, last], before, (1, 0)),
        (links.at[2:8, :, 0], after, (-1, 0)),
        (links.at[2:4, :, 0, 1], corner_x, (-1, 1)),
        (links.at[0:2, :, last, 0], corner_t, (1, -1)),
    )
    copies = [
        pltpu.make_async_remote_copy(
            src_ref=source,
            dst_ref=target,
            send_sem=send_sems.at[n],
            recv_sem=recv_sems.at[n],
            device_id=there(*step),
            device_id_type=MESH,
        )
        for n, (source, target, step) in enumerate(moves)
    ]
    for copy in copies:
        copy.start()
    for copy in copies:
        copy.wait()


def meet_all(ngx, devices, me):
    barrier = pltpu.get_barrier_semaphore()

    def greet(k, _):
        other = lax.rem(me + k, devices)
        pl.semaphore_signal(barrier, inc=1, device_id=(other // ngx, lax.rem(other, ngx)), device_id_type=MESH)
        return 0

    lax.fori_loop(1, devices, greet, 0)
    pl.semaphore_wait(barrier, devices - 1)


def exchange_kernel(nta, ngx, packed, fields, send_sems, recv_sems, own_sem):
    devices = nta * ngx
    me = lax.axis_index("ta") * ngx + lax.axis_index("gx")
    meet_all(ngx, devices, me)

    def move(k):
        other = lax.rem(me + k, devices)
        return pltpu.make_async_remote_copy(
            src_ref=packed.at[other],
            dst_ref=fields.at[me],
            send_sem=send_sems.at[k],
            recv_sem=recv_sems.at[k],
            device_id=(other // ngx, lax.rem(other, ngx)),
            device_id_type=MESH,
        )

    def start(k, _):
        move(k).start()
        return 0

    def wait(k, _):
        move(k).wait()
        return 0

    lax.fori_loop(1, devices, start, 0)
    own = pltpu.make_async_copy(packed.at[me], fields.at[me], own_sem)
    own.start()
    own.wait()
    lax.fori_loop(1, devices, wait, 0)


def total_kernel(nta, ngx, scale, part, total, row, slots_x, slots_t, sends_x, recvs_x, sends_t, recvs_t):
    ta, gx = lax.axis_index("ta"), lax.axis_index("gx")
    barrier = pltpu.get_barrier_semaphore()
    in_x = lambda k: (ta, lax.rem(gx + k, ngx))
    in_t = lambda k: (lax.rem(ta + k, nta), gx)

    def greet(peer):
        def one(k, _):
            pl.semaphore_signal(barrier, inc=1, device_id=peer(k), device_id_type=MESH)
            return 0

        return one

    lax.fori_loop(1, ngx, greet(in_x), 0)
    lax.fori_loop(1, nta, greet(in_t), 0)
    pl.semaphore_wait(barrier, ngx + nta - 2)

    def gather(source, slots, mine, count, peer, sends, recvs):
        def move(k):
            return pltpu.make_async_remote_copy(
                src_ref=source,
                dst_ref=slots.at[mine],
                send_sem=sends.at[k],
                recv_sem=recvs.at[k],
                device_id=peer(k),
                device_id_type=MESH,
            )

        def start(k, _):
            move(k).start()
            return 0

        def wait(k, _):
            move(k).wait()
            return 0

        lax.fori_loop(1, count, start, 0)
        slots[mine] = source[...]
        lax.fori_loop(1, count, wait, 0)
        return jnp.sum(slots[...], axis=0)

    row[...] = gather(part, slots_x, gx, ngx, in_x, sends_x, recvs_x)
    summed = gather(row, slots_t, ta, nta, in_t, sends_t, recvs_t) * scale
    total[...] = summed[:LEVELS, :TMAX]


def body(links):
    nta, ngx = lax.axis_size("ta"), lax.axis_size("gx")
    devices = nta * ngx
    slices = links.shape[4]
    vmem = pl.BlockSpec(memory_space=pltpu.VMEM)
    anywhere = pl.BlockSpec(memory_space=pl.ANY)
    array = lambda *shape: jax.ShapeDtypeStruct(shape, jnp.float32)
    sems = pltpu.SemaphoreType.DMA
    remote = lambda n: pltpu.CompilerParams(collective_id=n, has_side_effects=True, vmem_limit_bytes=8 * 2**20)

    halos = pl.pallas_call(
        lambda *refs: halo_kernel(nta, ngx, slices, *refs),
        out_shape=(
            array(8, 6, slices, 1, LANES),
            array(6, 6, slices, 1, LANES),
            array(8, 9, 2, 1, LANES),
            array(6, 9, 2, 1, LANES),
            array(2, 9, 1, LANES),
            array(2, 9, 1, LANES),
        ),
        in_specs=[anywhere],
        out_specs=(vmem,) * 6,
        scratch_shapes=[
            pltpu.VMEM((8, 6, slices, 1, LANES), jnp.float32),
            pltpu.VMEM((6, 6, slices, 1, LANES), jnp.float32),
            sems((3,)),
            sems((6,)),
            sems((6,)),
        ],
        compiler_params=remote(0),
        name="halos",
    )(links.reshape(8, 9, slices, 2, 1, LANES))
    shapes = ((48, slices, LANES), (36, slices, LANES), (72, 2, LANES), (54, 2, LANES), (18, 1, LANES), (18, 1, LANES))
    halos = [v.reshape(shape) for v, shape in zip(halos, shapes)]

    split = LANES // devices
    rows = 2 * slices
    width = rows * split
    flowed, packed = pl.pallas_call(
        lambda *refs: flow_kernel(slices, split, *refs),
        out_shape=(array(72, rows, LANES), array(36 * devices, width)),
        in_specs=[vmem] * 7,
        out_specs=(vmem, vmem),
        scratch_shapes=[
            pltpu.VMEM((72, 4, TOP + slices + 8, LANES), jnp.float32),
            pltpu.VMEM((72, 8, LANES), jnp.float32),
            pltpu.VMEM((72, 2, slices, LANES), jnp.float32),
            pltpu.VMEM((width, LANES), jnp.float32),
        ],
        compiler_params=pltpu.CompilerParams(vmem_limit_bytes=24 * 2**20),
        name="flow",
    )(links.reshape(72, rows, LANES), *halos)

    fields = pl.pallas_call(
        lambda *refs: exchange_kernel(nta, ngx, *refs),
        out_shape=array(devices, 36, 1, width),
        in_specs=[vmem],
        out_specs=vmem,
        scratch_shapes=[sems((devices,)), sems((devices,)), sems],
        compiler_params=remote(1),
        name="exchange",
    )(packed.reshape(devices, 36, 1, width))
    repeats = LANES // width
    fields = fields.reshape(devices * 36, width)
    if repeats > 1:
        fields = jnp.tile(fields, (1, repeats))
    part = pl.pallas_call(
        lambda *refs: loop_kernel(nta, 2 * split, *refs),
        out_shape=array(TMAX, LANES),
        in_specs=[vmem],
        out_specs=vmem,
        scratch_shapes=[
            pltpu.VMEM((36, nta, ngx, LANES), jnp.float32),
            pltpu.VMEM((TMAX, 18, nta * (ngx // 8), 8, LANES), jnp.float32),
            pltpu.VMEM((LEVELS, 18, nta, ngx, LANES), jnp.float32),
            pltpu.VMEM((LEVELS, 18, nta, ngx, LANES), jnp.float32),
        ],
        compiler_params=pltpu.CompilerParams(vmem_limit_bytes=24 * 2**20),
        name="loops",
    )(fields)
    scale = 1.0 / (3.0 * slices * nta * 2 * ngx * LANES * repeats)
    total = pl.pallas_call(
        lambda *refs: total_kernel(nta, ngx, scale, *refs),
        out_shape=array(LEVELS, TMAX),
        in_specs=[vmem],
        out_specs=vmem,
        scratch_shapes=[
            pltpu.VMEM((8, LANES), jnp.float32),
            pltpu.VMEM((ngx, 8, LANES), jnp.float32),
            pltpu.VMEM((nta, 8, LANES), jnp.float32),
            sems((ngx,)),
            sems((ngx,)),
            sems((nta,)),
            sems((nta,)),
        ],
        compiler_params=remote(2),
        name="total",
    )(part)
    return flowed.reshape(links.shape), total


def solution(mesh):
    spec = P(None, None, None, None, "ta", "gx", None)
    return jax.shard_map(body, mesh=mesh, in_specs=(spec,), out_specs=(spec, P()), check_vma=False)
```

```python
import jax
import jax.numpy as jnp
from jax import lax
from jax.experimental import pallas as pl
from jax.experimental.pallas import tpu as pltpu
from jax.sharding import PartitionSpec as P

NY = 4
NZ = 32
LANES = NY * NZ
TMAX = 8
LEVELS = 5
EPS_FLOW = 0.05
TOP = 8


def product(a, b, da=False, db=False):
    out = []
    for i in range(3):
        row = []
        for j in range(3):
            rr = ii = ri = ir = None
            for k in range(3):
                ar, ai = a[k][i] if da else a[i][k]
                br, bi = b[j][k] if db else b[k][j]
                t = (ar * br, ai * bi, ar * bi, ai * br)
                if rr is None:
                    rr, ii, ri, ir = t
                else:
                    rr, ii, ri, ir = rr + t[0], ii + t[1], ri + t[2], ir + t[3]
            re = rr - ii if da == db else rr + ii
            if da and db:
                im = -(ri + ir)
            elif da:
                im = ri - ir
            elif db:
                im = ir - ri
            else:
                im = ri + ir
            row.append((re, im))
        out.append(row)
    return out


def cmul(a, b):
    return (a[0] * b[0] - a[1] * b[1], a[0] * b[1] + a[1] * b[0])


def third_row(first, second):
    out = []
    for j in range(3):
        k, l = (j + 1) % 3, (j + 2) % 3
        x, y = cmul(first[k], second[l]), cmul(first[l], second[k])
        out.append((x[0] - y[0], y[1] - x[1]))
    return out


def evolve(link, staple):
    m = product(link, staple)
    half = -0.5 * EPS_FLOW
    d = [-EPS_FLOW * m[i][i][1] for i in range(3)]
    trace = (d[0] + d[1] + d[2]) * (1.0 / 3.0)
    d = [v - trace for v in d]
    off = {}
    for i, j in ((0, 1), (0, 2), (1, 2)):
        off[i, j] = (half * (m[i][j][0] - m[j][i][0]), half * (m[i][j][1] + m[j][i][1]))
    a, b, c = off[0, 1], off[0, 2], off[1, 2]
    na, nb, nc = (v[0] * v[0] + v[1] * v[1] for v in (a, b, c))
    s = [-(d[0] * d[0] + na + nb), -(d[1] * d[1] + na + nc), -(d[2] * d[2] + nb + nc)]
    p = -0.5 * (s[0] + s[1] + s[2])

    def times_i(w, v):
        return (-w * v[1], w * v[0])

    conj = lambda v: (v[0], -v[1])
    add = lambda u, v: (u[0] + v[0], u[1] + v[1])
    sub = lambda u, v: (u[0] - v[0], u[1] - v[1])
    sq = {
        (0, 1): sub(times_i(d[0] + d[1], a), cmul(b, conj(c))),
        (0, 2): add(times_i(d[0] + d[2], b), cmul(a, c)),
        (1, 2): sub(times_i(d[1] + d[2], c), cmul(conj(a), b)),
    }
    cube = s[0] * d[0] + s[1] * d[1] + s[2] * d[2]
    for key in sq:
        u, v = sq[key], off[key]
        cube = cube - 2.0 * (u[1] * v[0] - u[0] * v[1])
    delta = cube * (1.0 / 3.0)
    e0 = (1.0 - delta * delta * (1.0 / 720.0), delta * (1.0 / 6.0 - p * (1.0 / 120.0)))
    e1 = (1.0 - p * (1.0 / 6.0 - p * (1.0 / 120.0)), delta * (1.0 / 24.0 - p * (1.0 / 360.0)))
    e2 = (0.5 - p * (1.0 / 24.0 - p * (1.0 / 720.0)), delta * (1.0 / 120.0))
    e = [[None] * 3 for _ in range(3)]
    for i in range(3):
        e[i][i] = (e0[0] - e1[1] * d[i] + e2[0] * s[i], e0[1] + e1[0] * d[i] + e2[1] * s[i])
    for i, j in off:
        e[i][j] = add(cmul(e1, off[i, j]), cmul(e2, sq[i, j]))
        x = off[i, j]
        e[j][i] = add(cmul(e1, (-x[0], x[1])), cmul(e2, conj(sq[i, j])))
    return product(e, link)


def roll(v, by, axis=1):
    by = by % v.shape[axis]
    return v if by == 0 else pltpu.roll(v, by, axis)


def shift_y(v, by):
    return roll(v, -NZ * by)


def shift_z(v, by, z):
    if by == 1:
        return jnp.where(z < NZ - 1, roll(v, -1), roll(v, NZ - 1))
    return jnp.where(z > 0, roll(v, 1), roll(v, 1 - NZ))


def flow_kernel(slices, split, links, left, right, before, after, corner_x, corner_t, out, packed, pad, sums, done, turn):
    halves = slices // 8
    end = TOP + slices

    def fill(c, _):
        for p in range(2):
            for h in range(halves):
                pad[c, 1 + p, TOP + 8 * h : TOP + 8 * h + 8, :] = links[c, pl.ds(16 * h + p, 8, stride=2), :]
            pad[c, 1 + p, TOP - 1 : TOP, :] = before[c, p : p + 1, :]
        return 0

    lax.fori_loop(0, 72, fill, 0)

    def fill_after(c, _):
        for p in range(2):
            pad[18 + c, 1 + p, end : end + 1, :] = after[c, p : p + 1, :]
        return 0

    lax.fori_loop(0, 54, fill_after, 0)

    def fill_corner(c, _):
        pad[18 + c, 0, end : end + 1, :] = corner_x[c, 0:1, :]
        pad[c, 3, TOP - 1 : TOP, :] = corner_t[c, 0:1, :]
        return 0

    lax.fori_loop(0, 18, fill_corner, 0)
    for source, plane, dirs in ((left, 0, (0, 1, 2, 3)), (right, 3, (0, 2, 3))):
        for n, d in enumerate(dirs):
            for h in range(halves):
                rows = [
                    [
                        tuple(source[12 * n + 6 * ri + 3 * i + j, 8 * h : 8 * h + 8, :] for ri in range(2))
                        for j in range(3)
                    ]
                    for i in range(2)
                ]
                rows.append(third_row(rows[0], rows[1]))
                for i in range(3):
                    for j in range(3):
                        for ri in range(2):
                            pad[18 * d + 9 * ri + 3 * i + j, plane, TOP + 8 * h : TOP + 8 * h + 8, :] = rows[i][j][ri]

    lane = lax.broadcasted_iota(jnp.int32, (8, LANES), 1)
    z = lane & (NZ - 1)

    def chunk(p, h):
        def load(d, *steps):
            dt = dx = 0
            rolls = []
            for axis, by in steps:
                if axis == 0:
                    dt += by
                elif axis == 1:
                    dx += by
                else:
                    rolls.append((axis, by))

            def one(c):
                v = pad[c, 1 + p + dx, TOP + 8 * h + dt : TOP + 8 * h + dt + 8, :]
                for axis, by in rolls:
                    v = shift_y(v, by) if axis == 2 else shift_z(v, by, z)
                return v

            return [[(one(18 * d + 3 * i + j), one(18 * d + 9 + 3 * i + j)) for j in range(3)] for i in range(3)]

        seen = set()

        def collect(d, value):
            for i in range(3):
                for j in range(3):
                    for ri in range(2):
                        at = 18 * d + 9 * ri + 3 * i + j
                        if at in seen:
                            sums[at] = sums[at] + value[i][j][ri]
                        else:
                            seen.add(at)
                            sums[at] = value[i][j][ri]

        def lower(m, v):
            if v < 2:
                q = product(load(m, (v, -1)), load(v, (m, 1), (v, -1)))
                collect(m, product(q, load(v, (v, -1)), da=True))
            else:
                q = product(product(load(m), load(v, (m, 1))), load(v), da=True)
                move = (lambda w: shift_y(w, -1)) if v == 2 else (lambda w: shift_z(w, -1, z))
                collect(m, [[(move(e[0]), move(e[1])) for e in row] for row in q])

        for m in range(4):
            for v in range(m + 1, 4):
                w = product(load(v, (m, 1)), load(m, (v, 1)), db=True)
                collect(m, product(w, load(v), db=True))
                collect(v, product(w, load(m), da=True, db=True))
                lower(m, v)
                lower(v, m)
        for m in range(4):
            staple = [
                [(sums[18 * m + 3 * i + j], sums[18 * m + 9 + 3 * i + j]) for j in range(3)] for i in range(3)
            ]
            new = evolve(load(m), staple)
            for i in range(3):
                for j in range(3):
                    for ri in range(2):
                        done[18 * m + 9 * ri + 3 * i + j, p, 8 * h : 8 * h + 8, :] = new[i][j][ri]

    def plane(p, _):
        for h in range(halves):
            chunk(p, h)
        return 0

    lax.fori_loop(0, 2, plane, 0)

    def back(c, _):
        for p in range(2):
            for h in range(halves):
                out[c, pl.ds(16 * h + p, 8, stride=2), :] = done[c, p, 8 * h : 8 * h + 8, :]
        return 0

    lax.fori_loop(0, 72, back, 0)

    width = LANES // split

    def pack(g, _):
        for p in range(2):
            for h in range(halves):
                held = [done[split * g + c, p, 8 * h : 8 * h + 8, :] for c in range(split)]
                for k in range(split):
                    mixed = None
                    for c in range(split):
                        moved = roll(held[c], width * (c - k))
                        mixed = moved if mixed is None else jnp.where(lane // width == c, moved, mixed)
                    turn[pl.ds(8 * 2 * split * h + 2 * k + p, 8, stride=2 * split), :] = mixed
        turned = jnp.transpose(turn[...])
        for c in range(split):
            packed[pl.ds(split * g + c, width, stride=36), :] = turned[width * c : width * c + width, :]
        return 0

    for g in range(36 // split):
        pack(g, 0)


def row_product(row, b):
    out = []
    for j in range(3):
        x = [cmul(row[k], b[k][j]) for k in range(3)]
        out.append((x[0][0] + x[1][0] + x[2][0], x[0][1] + x[1][1] + x[2][1]))
    return out


def loop_kernel(blocks, per_slice, slices, arrived, out, fields, reach, lines):
    groups = fields.shape[2]
    for b in range(blocks):
        for c in range(36):
            fields[c, b] = arrived[pl.ds(36 * groups * b + c, groups, stride=36), :]
    wide = lax.broadcasted_iota(jnp.int32, (groups, LANES), 1)
    odd = (wide & 1) == 1
    slot = (wide // per_slice) % slices
    lane = lax.broadcasted_iota(jnp.int32, (8, LANES), 1)
    row = lax.broadcasted_iota(jnp.int32, (8, LANES), 0)

    def matrix(get):
        return [[(get(3 * i + j), get(9 + 3 * i + j)) for j in range(3)] for i in range(3)]

    def forward_x(v, distance):
        if distance == 1:
            return jnp.where(odd, roll(roll(v, -1, 0), 1), roll(v, -1))
        return roll(v, -(distance // 2), 0)

    def forward_t(get, b, s):
        return roll(jnp.where(slot >= s, get(b), get(lax.rem(b + 1, blocks))), -per_slice * s)

    def temporal(b, _):
        held = matrix(lambda c: fields[c, b])
        for s in range(TMAX):
            if s:
                held = product(held, matrix(lambda c: forward_t(lambda at: fields[c, at], b, s)))
            for i in range(3):
                for j in range(3):
                    for ri in range(2):
                        reach[s, 9 * ri + 3 * i + j, b] = held[i][j][ri]
        return 0

    lax.fori_loop(0, blocks, temporal, 0)

    def first(b, _):
        for c in range(18):
            lines[0, c, b] = fields[18 + c, b]
        return 0

    lax.fori_loop(0, blocks, first, 0)
    out[...] = jnp.zeros((8, LANES), jnp.float32)
    for k in range(LEVELS):
        distance = 2**k

        def cell(b, totals):
            line = matrix(lambda c: lines[k, c, b])
            new = []
            for extent in range(1, TMAX + 1):
                near = matrix(lambda c: reach[extent - 1, c, b])
                far = [[tuple(forward_x(v, distance) for v in e) for e in r] for r in near]
                end = matrix(lambda c: forward_t(lambda at: lines[k, c, at], b, extent))
                total = totals[extent - 1]
                for i in range(3):
                    upper = row_product(line[i], far)
                    lower = row_product(near[i], end)
                    for u, v in zip(upper, lower):
                        total = total + (u[0] * v[0] + u[1] * v[1])
                new.append(total)
            return tuple(new)

        totals = lax.fori_loop(0, blocks, cell, (jnp.zeros((groups, LANES), jnp.float32),) * TMAX)
        block = jnp.concatenate([jnp.sum(t, axis=0, keepdims=True) for t in totals], axis=0)
        spread = jnp.where(lane == row, jnp.sum(block, axis=1, keepdims=True), 0.0)
        out[...] = jnp.where(row == k, jnp.sum(spread, axis=0, keepdims=True), out[...])
        if k + 1 < LEVELS:

            def grow(b, _):
                own = matrix(lambda c: lines[k, c, b])
                far = [[tuple(forward_x(v, distance) for v in e) for e in r] for r in own]
                new = product(own, far)
                for i in range(3):
                    for j in range(3):
                        for ri in range(2):
                            lines[k + 1, 9 * ri + 3 * i + j, b] = new[i][j][ri]
                return 0

            lax.fori_loop(0, blocks, grow, 0)


MESH = pl.DeviceIdType.MESH


def halo_kernel(nta, ngx, slices, links, left, right, before, after, corner_x, corner_t, last_plane, first_plane, local_sems, send_sems, recv_sems):
    ta, gx = lax.axis_index("ta"), lax.axis_index("gx")
    there = lambda dt, dx: (lax.rem(ta + dt + nta, nta), lax.rem(gx + dx + ngx, ngx))
    local = [
        pltpu.make_async_copy(source, target, local_sems.at[n])
        for n, (source, target) in enumerate(
            (
                (links.at[:, 0:6, :, 1], last_plane),
                (links.at[0:2, 0:6, :, 0], first_plane.at[0:2]),
                (links.at[4:8, 0:6, :, 0], first_plane.at[2:6]),
            )
        )
    ]
    for copy in local:
        copy.start()
    barrier = pltpu.get_barrier_semaphore()
    steps = ((0, 1), (0, -1), (1, 0), (-1, 0), (-1, 1), (1, -1))
    for step in steps:
        pl.semaphore_signal(barrier, inc=1, device_id=there(*step), device_id_type=MESH)
    pl.semaphore_wait(barrier, len(steps))
    last = slices - 1
    for copy in local:
        copy.wait()
    moves = (
        (last_plane, left, (0, 1)),
        (first_plane, right, (0, -1)),
        (links.at[:, :, last], before, (1, 0)),
        (links.at[2:8, :, 0], after, (-1, 0)),
        (links.at[2:4, :, 0, 1], corner_x, (-1, 1)),
        (links.at[0:2, :, last, 0], corner_t, (1, -1)),
    )
    copies = [
        pltpu.make_async_remote_copy(
            src_ref=source,
            dst_ref=target,
            send_sem=send_sems.at[n],
            recv_sem=recv_sems.at[n],
            device_id=there(*step),
            device_id_type=MESH,
        )
        for n, (source, target, step) in enumerate(moves)
    ]
    for copy in copies:
        copy.start()
    for copy in copies:
        copy.wait()


def meet_all(ngx, devices, me):
    barrier = pltpu.get_barrier_semaphore()

    def greet(k, _):
        other = lax.rem(me + k, devices)
        pl.semaphore_signal(barrier, inc=1, device_id=(other // ngx, lax.rem(other, ngx)), device_id_type=MESH)
        return 0

    lax.fori_loop(1, devices, greet, 0)
    pl.semaphore_wait(barrier, devices - 1)


def exchange_kernel(nta, ngx, packed, fields, send_sems, recv_sems, own_sem):
    devices = nta * ngx
    me = lax.axis_index("ta") * ngx + lax.axis_index("gx")
    meet_all(ngx, devices, me)

    def move(k):
        other = lax.rem(me + k, devices)
        return pltpu.make_async_remote_copy(
            src_ref=packed.at[other],
            dst_ref=fields.at[me],
            send_sem=send_sems.at[k],
            recv_sem=recv_sems.at[k],
            device_id=(other // ngx, lax.rem(other, ngx)),
            device_id_type=MESH,
        )

    def start(k, _):
        move(k).start()
        return 0

    def wait(k, _):
        move(k).wait()
        return 0

    lax.fori_loop(1, devices, start, 0)
    own = pltpu.make_async_copy(packed.at[me], fields.at[me], own_sem)
    own.start()
    own.wait()
    lax.fori_loop(1, devices, wait, 0)


def total_kernel(nta, ngx, scale, part, total, row, slots_x, slots_t, sends_x, recvs_x, sends_t, recvs_t):
    ta, gx = lax.axis_index("ta"), lax.axis_index("gx")
    barrier = pltpu.get_barrier_semaphore()
    in_x = lambda k: (ta, lax.rem(gx + k, ngx))
    in_t = lambda k: (lax.rem(ta + k, nta), gx)

    def greet(peer):
        def one(k, _):
            pl.semaphore_signal(barrier, inc=1, device_id=peer(k), device_id_type=MESH)
            return 0

        return one

    lax.fori_loop(1, ngx, greet(in_x), 0)
    lax.fori_loop(1, nta, greet(in_t), 0)
    pl.semaphore_wait(barrier, ngx + nta - 2)

    def gather(source, slots, mine, count, peer, sends, recvs):
        def move(k):
            return pltpu.make_async_remote_copy(
                src_ref=source,
                dst_ref=slots.at[mine],
                send_sem=sends.at[k],
                recv_sem=recvs.at[k],
                device_id=peer(k),
                device_id_type=MESH,
            )

        def start(k, _):
            move(k).start()
            return 0

        def wait(k, _):
            move(k).wait()
            return 0

        lax.fori_loop(1, count, start, 0)
        slots[mine] = source[...]
        lax.fori_loop(1, count, wait, 0)
        return jnp.sum(slots[...], axis=0)

    row[...] = gather(part, slots_x, gx, ngx, in_x, sends_x, recvs_x)
    summed = gather(row, slots_t, ta, nta, in_t, sends_t, recvs_t) * scale
    total[...] = summed[:LEVELS, :TMAX]


def body(links):
    nta, ngx = lax.axis_size("ta"), lax.axis_size("gx")
    devices = nta * ngx
    slices = links.shape[4]
    vmem = pl.BlockSpec(memory_space=pltpu.VMEM)
    anywhere = pl.BlockSpec(memory_space=pl.ANY)
    array = lambda *shape: jax.ShapeDtypeStruct(shape, jnp.float32)
    sems = pltpu.SemaphoreType.DMA
    remote = lambda n: pltpu.CompilerParams(collective_id=n, has_side_effects=True, vmem_limit_bytes=8 * 2**20)

    halos = pl.pallas_call(
        lambda *refs: halo_kernel(nta, ngx, slices, *refs),
        out_shape=(
            array(8, 6, slices, 1, LANES),
            array(6, 6, slices, 1, LANES),
            array(8, 9, 2, 1, LANES),
            array(6, 9, 2, 1, LANES),
            array(2, 9, 1, LANES),
            array(2, 9, 1, LANES),
        ),
        in_specs=[anywhere],
        out_specs=(vmem,) * 6,
        scratch_shapes=[
            pltpu.VMEM((8, 6, slices, 1, LANES), jnp.float32),
            pltpu.VMEM((6, 6, slices, 1, LANES), jnp.float32),
            sems((3,)),
            sems((6,)),
            sems((6,)),
        ],
        compiler_params=remote(0),
        name="halos",
    )(links.reshape(8, 9, slices, 2, 1, LANES))
    shapes = ((48, slices, LANES), (36, slices, LANES), (72, 2, LANES), (54, 2, LANES), (18, 1, LANES), (18, 1, LANES))
    halos = [v.reshape(shape) for v, shape in zip(halos, shapes)]

    split = LANES // devices
    rows = 2 * slices
    width = rows * split
    flowed, packed = pl.pallas_call(
        lambda *refs: flow_kernel(slices, split, *refs),
        out_shape=(array(72, rows, LANES), array(36 * devices, width)),
        in_specs=[vmem] * 7,
        out_specs=(vmem, vmem),
        scratch_shapes=[
            pltpu.VMEM((72, 4, TOP + slices + 8, LANES), jnp.float32),
            pltpu.VMEM((72, 8, LANES), jnp.float32),
            pltpu.VMEM((72, 2, slices, LANES), jnp.float32),
            pltpu.VMEM((width, LANES), jnp.float32),
        ],
        compiler_params=pltpu.CompilerParams(vmem_limit_bytes=24 * 2**20),
        name="flow",
    )(links.reshape(72, rows, LANES), *halos)

    fields = pl.pallas_call(
        lambda *refs: exchange_kernel(nta, ngx, *refs),
        out_shape=array(devices, 36, 1, width),
        in_specs=[vmem],
        out_specs=vmem,
        scratch_shapes=[sems((devices,)), sems((devices,)), sems],
        compiler_params=remote(1),
        name="exchange",
    )(packed.reshape(devices, 36, 1, width))
    repeats = LANES // width
    fields = fields.reshape(devices * 36, width)
    if repeats > 1:
        fields = jnp.tile(fields, (1, repeats))
    part = pl.pallas_call(
        lambda *refs: loop_kernel(nta, 2 * split, slices, *refs),
        out_shape=array(TMAX, LANES),
        in_specs=[vmem],
        out_specs=vmem,
        scratch_shapes=[
            pltpu.VMEM((36, nta, ngx, LANES), jnp.float32),
            pltpu.VMEM((TMAX, 18, nta, ngx, LANES), jnp.float32),
            pltpu.VMEM((LEVELS, 18, nta, ngx, LANES), jnp.float32),
        ],
        compiler_params=pltpu.CompilerParams(vmem_limit_bytes=24 * 2**20),
        name="loops",
    )(fields)
    scale = 1.0 / (3.0 * slices * nta * 2 * ngx * LANES * repeats)
    total = pl.pallas_call(
        lambda *refs: total_kernel(nta, ngx, scale, *refs),
        out_shape=array(LEVELS, TMAX),
        in_specs=[vmem],
        out_specs=vmem,
        scratch_shapes=[
            pltpu.VMEM((8, LANES), jnp.float32),
            pltpu.VMEM((ngx, 8, LANES), jnp.float32),
            pltpu.VMEM((nta, 8, LANES), jnp.float32),
            sems((ngx,)),
            sems((ngx,)),
            sems((nta,)),
            sems((nta,)),
        ],
        compiler_params=remote(2),
        name="total",
    )(part)
    return flowed.reshape(links.shape), total


def solution(mesh):
    spec = P(None, None, None, None, "ta", "gx", None)
    return jax.shard_map(body, mesh=mesh, in_specs=(spec,), out_specs=(spec, P()), check_vma=False)
```
